32 devices in a mesh: req: 4 (over y, x), head: 8 (over z, core).
Axes of the slice: x: 2, y: 2, z: 4, core: 2. Of those that a mesh axis runs over, the one named last changes fastest.
Arguments:
- hidden_in: bfloat16 [2048, 2048], P(('req', 'head')), may hold values from -6 to 6
- queries: bfloat16 [2048, 2048], P(('req', 'head')), may hold values from -160 to 160
- keys_values: bfloat16 [2048, 1024], P(('req', 'head')), may hold values from -10 to 10
- request_of_row: int32 [2048], P('req'), may hold values from 0 to 7, as said below
- page_route: int32 [4, 8, 4], P('req', 'head'), may hold values from 0 to 3, each once within a row
- expert_ids: int32 [2048, 6], P(('req', 'head')), may hold values from 0 to 31, all different within a row; in each aligned block of 64 rows (0 to 63, 64 to 127, ...) at most 14 rows name the same one
- expert_weights: float32 [2048, 6], P(('req', 'head')), may hold values from 0.05 to 0.5
- norm_gain: float32 [2048], replicated, may hold values from 0.25 to 1.75
- shared_gate_up: bfloat16 [2048, 2, 1408], replicated, may hold values from -0.125 to 0.125
- shared_down: bfloat16 [1408, 2048], replicated, may hold values from -0.15625 to 0.15625
- expert_gate_up: bfloat16 [32, 2, 1408, 2048], P('head', None, 'req'), may hold values from -0.125 to 0.125
- expert_down: bfloat16 [32, 1408, 2048], P('head', 'req'), may hold values from -0.15625 to 0.15625
Outputs:
- layer_out: bfloat16 [2048, 2048], P(('req', 'head'))
The draws below stay inside these ranges and needn't reach their ends.
Inputs may be any that keep to these rules, and one draw needn't show every extreme that they name: `request_of_row`: each group of 512 rows g holds two requests, ids 2 g then 2 g + 1, each a whole number of pages of 16 rows and at least 32 rows long. `page_route`: for every device, the groups receiving its pages form a permutation of all groups. `expert_ids`: each row names 6 different experts; among the rows of one device no expert is named more than 14 times, and some device names some expert exactly 14 times.
All inputs are finite; a program needn't handle non-finite values.
Results may differ from the reference program's by a relative error of at most 0.006.
Values may be sent and summed in bfloat16 or wider, within the bound.
A program may use at most 192 MiB of HBM per device.

```python
import math
import jax
import jax.numpy as jnp
import numpy as np
from jax import lax

D = 2048
QUERY_HEADS = 16
KEY_VALUE_HEADS = 4
HEAD_SIZE = 128
FF = 1408
SFF = 1408
EXPERTS = 32
TOP = 6
TOK_DEV = 64
PAGE = 16
CAP = 14
GROUP_TOKENS = 512
TOKEN_TOTAL = 2048
N_REQ = 4
N_HEAD = 8


def attention_inputs(key):
    query_key = jax.random.fold_in(key, 101)
    pair_random_key = jax.random.fold_in(key, 102)
    query_draw = jnp.clip(jax.random.normal(query_key, (TOKEN_TOTAL, QUERY_HEADS * HEAD_SIZE), jnp.float32), -6.0, 6.0)
    pair_sample = jnp.clip(jax.random.normal(pair_random_key, (TOKEN_TOTAL, 2 * KEY_VALUE_HEADS * HEAD_SIZE), jnp.float32), -6.0, 6.0)
    return (query_draw, pair_sample)


def draw_queries(key, part):
    return attention_inputs(key)[0].astype(jnp.bfloat16)


def draw_keys_values(key, part):
    return attention_inputs(key)[1].astype(jnp.bfloat16)


def draw_request_of_row(key, part):
    pages_group = GROUP_TOKENS // PAGE
    split_page = jax.random.randint(jax.random.fold_in(key, 105), (TOKEN_TOTAL // GROUP_TOKENS, 1), pages_group // 16, pages_group - pages_group // 16 + 1)
    page_index = jnp.arange(GROUP_TOKENS, dtype=jnp.int32)[None, :] // PAGE
    group_index = jnp.arange(TOKEN_TOTAL // GROUP_TOKENS, dtype=jnp.int32)[:, None]
    return (2 * group_index + (page_index >= split_page).astype(jnp.int32)).reshape(TOKEN_TOTAL).astype(jnp.int32)


def block_levels(stream_key, dims, cuts, smallest, high):
    def one(dim, blocks):
        heights = jax.random.uniform(jax.random.fold_in(jax.random.fold_in(stream_key, 6), dim), (blocks,), jnp.float32, smallest / len(cuts), high / len(cuts))
        return jnp.repeat(jnp.exp(heights), dims[dim] // blocks).reshape((-1,) + (1,) * (len(dims) - dim - 1))

    level = one(*cuts[0])
    for cut in cuts[1:]:
        level = level * one(*cut)
    return level


def routed_block(key, own, number, rows, amount, top, bound, lean):
    sequence = jax.random.permutation(key, amount)
    heavy_load, ordinary = shares(amount, rows * top, bound, lean, True), shares(amount, rows * top, bound, lean, False)
    places = jnp.arange(amount)

    def named(tallies, offset_by):
        used = int((tallies > 0).sum())
        fixed = max(1, used // 4)
        shifted = fixed + (places - fixed + offset_by * (used - fixed)) % max(1, amount - fixed)
        return jnp.zeros((amount,), jnp.int32).at[sequence[jnp.where(places < fixed, places, shifted)]].set(jnp.asarray(tallies, jnp.int32))

    tallies = jnp.where(number % 4 == 0, named(heavy_load, number // 4), named(ordinary, number - number // 4 - 1))
    mixed = jax.random.permutation(jax.random.fold_in(own, 3), amount)
    giver, sink = mixed[0:amount // 2 * 2:2], mixed[1:amount // 2 * 2:2]
    room = jnp.minimum(tallies[giver] - 1, bound - tallies[sink]) // 2
    room = jnp.where((giver == sequence[0]) | (sink == sequence[0]) | (tallies[sink] == 0), 0, jnp.maximum(room, 0))
    shifted = jax.random.randint(jax.random.fold_in(own, 4), (amount // 2,), 0, 1 << 20) % (room + 1)
    tallies = tallies.at[giver].add(-shifted).at[sink].add(shifted)
    members = jnp.searchsorted(jnp.cumsum(tallies), jnp.arange(rows * top), side="right").astype(jnp.int32)
    listing = members.reshape(top, rows).T
    listing = listing[jax.random.permutation(jax.random.fold_in(own, 1), rows)]
    offset_by = jax.random.randint(jax.random.fold_in(own, 2), (rows, 1), 0, top)
    return jnp.take_along_axis(listing, (jnp.arange(top)[None, :] + offset_by) % top, axis=1)


def shares(count, total, limit, slope, full):
    loads = [(1 << 20) // math.isqrt(standing ** slope) + 1 for standing in range(1, count + 1)]
    largest = limit if full else min(limit, max(-(-total // count), total * loads[0] // sum(loads)))
    least = 1 if total - largest >= count - 1 else 0
    given, rest = [largest] + [least] * (count - 1), total - largest - least * (count - 1)
    while rest > 0:
        candidates = [i for i in range(1, count) if given[i] < largest] or [i for i in range(1, count) if given[i] < limit]
        mass, budget = sum([loads[i] for i in candidates]), rest
        for i in candidates:
            addition = min(limit - given[i], max(1, budget * loads[i] // mass), rest)
            given[i] = given[i] + addition
            rest = rest - addition
    return np.array(given)


def gaussian(own_key, extent, scale, reach, shards=(), kind=jnp.bfloat16):
    entries = scale * jax.random.normal(own_key, extent, jnp.float32)
    if shards:
        entries = entries * block_levels(own_key, extent, shards, -0.22, 0.18)
    return jnp.clip(entries, -reach, reach).astype(kind)


def setup_inputs(seed: int = 0) -> dict:
    streams_of = jax.random.split(jax.random.key(seed), 13)
    hidden_in = gaussian(streams_of[0], (TOKEN_TOTAL, D), 1.0, 6.0, ((0, 32),))
    queries = draw_queries(jax.random.fold_in(streams_of[12], 71), 0)
    keys_values = draw_keys_values(jax.random.fold_in(streams_of[12], 71), 0)
    request_of_row = draw_request_of_row(jax.random.fold_in(streams_of[12], 71), 0)
    page_route = jax.vmap(lambda own: jax.random.permutation(own, N_REQ))(jax.random.split(streams_of[4], N_REQ * N_HEAD)).reshape((N_REQ, N_HEAD, N_REQ)).astype(jnp.int32)
    expert_ids_keys = jax.random.split(jax.random.fold_in(streams_of[5], 1), TOKEN_TOTAL // TOK_DEV)
    expert_ids_turns = jax.random.permutation(jax.random.fold_in(streams_of[5], 3), TOKEN_TOTAL // TOK_DEV)
    expert_ids = jax.vmap(lambda own, number: routed_block(jax.random.fold_in(streams_of[5], 2), own, number, TOK_DEV, EXPERTS, TOP, CAP, 1))(expert_ids_keys, expert_ids_turns).reshape((TOKEN_TOTAL, TOP))
    expert_weights = jnp.clip(jnp.exp(math.log(0.5) - 2.3025851 * jax.random.uniform(streams_of[6], (TOKEN_TOTAL, TOP), jnp.float32) ** block_levels(streams_of[6], (TOKEN_TOTAL, TOP), ((0, 32),), -0.2, 0.2)), 0.05, 0.5)
    norm_gain = jnp.clip(1.0 + 0.15 * jax.random.normal(streams_of[7], (D,), jnp.float32), 0.25, 1.75)
    shared_gate_up = gaussian(streams_of[8], (D, 2, SFF), D ** -0.5, 0.125)
    shared_down = gaussian(streams_of[9], (SFF, D), SFF ** -0.5, 0.15625)
    expert_gate_up = gaussian(streams_of[10], (EXPERTS, 2, FF, D), D ** -0.5, 0.125, ((0, 8), (2, 4)))
    expert_down = gaussian(streams_of[11], (EXPERTS, FF, D), FF ** -0.5, 0.15625, ((0, 8), (1, 4)))
    return {"hidden_in": hidden_in, "queries": queries, "keys_values": keys_values, "request_of_row": request_of_row, "page_route": page_route, "expert_ids": expert_ids, "expert_weights": expert_weights, "norm_gain": norm_gain, "shared_gate_up": shared_gate_up, "shared_down": shared_down, "expert_gate_up": expert_gate_up, "expert_down": expert_down}


negative_large = -1e+30

def silu_mul(gate_value, upward):
    return gate_value / (1.0 + jnp.exp(-gate_value)) * upward

def source_rows(page_route):
    rows_all = jnp.arange(TOKEN_TOTAL, dtype=jnp.int32)
    group_of = rows_all // GROUP_TOKENS
    column_of = rows_all // TOK_DEV % N_HEAD
    page_slot = rows_all % TOK_DEV // PAGE
    within_page = rows_all % PAGE
    targets = page_route[page_slot, column_of]
    matches = (targets == group_of[:, None]).astype(jnp.int32)
    source_page = lax.optimization_barrier(jnp.sum(matches * jnp.arange(N_REQ, dtype=jnp.int32)[None, :], axis=1))
    return ((page_slot * N_HEAD + column_of) * TOK_DEV + source_page * PAGE + within_page).astype(jnp.int32)

def attend_group(inputs):
    query_group, group_of_pair, segment_group = inputs
    position = jnp.arange(GROUP_TOKENS, dtype=jnp.int32)
    allowed = (segment_group[:, None] == segment_group[None, :]) & (position[None, :] <= position[:, None])
    group_fraction = QUERY_HEADS // KEY_VALUE_HEADS
    score_scale = HEAD_SIZE ** (-0.5)

    def one_head(head_index):
        query_head = lax.dynamic_slice_in_dim(query_group, head_index * HEAD_SIZE, HEAD_SIZE, 1)
        index_of_pair = head_index // group_fraction
        key_head = lax.dynamic_slice_in_dim(group_of_pair, index_of_pair * HEAD_SIZE, HEAD_SIZE, 1)
        head_values = lax.dynamic_slice_in_dim(group_of_pair, KEY_VALUE_HEADS * HEAD_SIZE + index_of_pair * HEAD_SIZE, HEAD_SIZE, 1)
        score = jnp.dot(query_head, key_head.T, preferred_element_type=jnp.float32) * score_scale
        masked = jnp.where(allowed, score, negative_large)
        top_score = lax.optimization_barrier(jnp.max(masked, axis=1, keepdims=True))
        weights = jnp.where(allowed, jnp.exp(masked - top_score), 0.0)
        row_total = lax.optimization_barrier(jnp.sum(weights, axis=1, keepdims=True))
        return jnp.dot(weights.astype(jnp.bfloat16), head_values, preferred_element_type=jnp.float32) / row_total
    heads_out = lax.map(one_head, jnp.arange(QUERY_HEADS, dtype=jnp.int32))
    return jnp.transpose(heads_out, (1, 0, 2)).reshape(GROUP_TOKENS, QUERY_HEADS * HEAD_SIZE)

def reference(hidden_in, queries, keys_values, request_of_row, page_route, expert_ids, expert_weights, norm_gain, shared_gate_up, shared_down, expert_gate_up, expert_down):
    source = source_rows(page_route)
    resid = jnp.take(hidden_in, source, axis=0)
    rows_of_queries = jnp.take(queries, source, axis=0)
    key_value_rows = jnp.take(keys_values, source, axis=0)
    grouped_rows = (rows_of_queries.reshape(N_REQ, GROUP_TOKENS, QUERY_HEADS * HEAD_SIZE), key_value_rows.reshape(N_REQ, GROUP_TOKENS, 2 * KEY_VALUE_HEADS * HEAD_SIZE), request_of_row.reshape(N_REQ, GROUP_TOKENS))
    context = lax.map(attend_group, grouped_rows).reshape(TOKEN_TOTAL, QUERY_HEADS * HEAD_SIZE)
    mixed_rows = resid.astype(jnp.float32) + context
    mean_square = lax.optimization_barrier(jnp.mean(mixed_rows * mixed_rows, axis=1, keepdims=True))
    normed = (mixed_rows * lax.rsqrt(mean_square + 1e-06) * norm_gain).astype(jnp.bfloat16)
    shared_both = jnp.dot(normed, shared_gate_up.reshape(D, 2 * SFF), preferred_element_type=jnp.float32).reshape(TOKEN_TOTAL, 2, SFF)
    shared_hidden = silu_mul(shared_both[:, 0], shared_both[:, 1]).astype(jnp.bfloat16)
    shared_out = jnp.dot(shared_hidden, shared_down, preferred_element_type=jnp.float32)
    flat_experts = expert_ids.reshape(-1)
    flat_weights = expert_weights.reshape(-1)
    most_rows = N_REQ * N_HEAD * CAP
    part_width = FF // N_REQ

    def one_expert(routed, expert):
        hit_mask = flat_experts == expert
        index_of_pair = jnp.nonzero(hit_mask, size=most_rows, fill_value=0)[0].astype(jnp.int32)
        live_rows = jnp.arange(most_rows, dtype=jnp.int32) < jnp.sum(hit_mask.astype(jnp.int32))
        token_of = (index_of_pair // TOP).astype(jnp.int32)
        rows_in = jnp.take(normed, token_of, axis=0)
        gate_up = lax.dynamic_index_in_dim(expert_gate_up, expert, 0, keepdims=False)
        down_matrix = lax.dynamic_index_in_dim(expert_down, expert, 0, keepdims=False)
        gate_value = jnp.dot(rows_in, gate_up[0].T, preferred_element_type=jnp.float32)
        upward = jnp.dot(rows_in, gate_up[1].T, preferred_element_type=jnp.float32)
        hidden = silu_mul(gate_value, upward).astype(jnp.bfloat16)
        result = jnp.zeros((most_rows, D), jnp.float32)
        for quarter in range(N_REQ):
            part_out = jnp.dot(hidden[:, quarter * part_width:(quarter + 1) * part_width], down_matrix[quarter * part_width:(quarter + 1) * part_width], preferred_element_type=jnp.float32).astype(jnp.bfloat16)
            result = result + lax.optimization_barrier(part_out).astype(jnp.float32)
        scaled = result * jnp.where(live_rows, jnp.take(flat_weights, index_of_pair), 0.0)[:, None]
        return (routed.at[token_of].add(scaled), None)
    routed = lax.scan(one_expert, jnp.zeros((TOKEN_TOTAL, D), jnp.float32), jnp.arange(EXPERTS, dtype=jnp.int32))[0]
    return (mixed_rows + shared_out + routed).astype(jnp.bfloat16)
```

```python
import jax
import jax.numpy as jnp
from jax import lax
from jax.sharding import PartitionSpec as P

QUERY_HEADS = 16
KEY_VALUE_HEADS = 4
HEAD_SIZE = 128
EXPERTS = 32
TOP = 6
CAP = 14


negative_large = -1e30


def silu_mul(gate_value, upward):
    return gate_value / (1.0 + jnp.exp(-gate_value)) * upward


def slot_tables(expert_ids, expert_weights, local_experts, token_rows, devices):
    all_ids = lax.all_gather(expert_ids, ("req", "head"), axis=0, tiled=True)
    all_weights = lax.all_gather(expert_weights, ("req", "head"), axis=0, tiled=True)
    first = lax.axis_index("head") * local_experts
    mine = first + jnp.arange(local_experts, dtype=jnp.int32)
    hit = all_ids[:, :, None] == mine[None, None, :]
    pair_weight = jnp.sum(jnp.where(hit, all_weights[:, :, None], 0.0), axis=1)
    named = jnp.any(hit, axis=1).reshape(devices, token_rows, local_experts)
    before = jnp.tril(jnp.ones((token_rows, token_rows), jnp.bfloat16), -1)
    rank = jnp.einsum(
        "ut,dtj->duj", before, named.astype(jnp.bfloat16), preferred_element_type=jnp.float32
    ).astype(jnp.int32)
    joined = 4
    blocks = devices // joined
    place = jnp.arange(devices, dtype=jnp.int32)[:, None, None] % joined * CAP + rank
    place = jnp.where(named, place, -1).reshape(blocks, joined * token_rows, local_experts)
    place = jnp.transpose(place, (0, 2, 1))
    slots = jnp.arange(joined * CAP, dtype=jnp.int32)
    placing = place[:, :, None, :] == slots[None, None, :, None]
    pair_weight = jnp.transpose(
        pair_weight.reshape(blocks, joined * token_rows, local_experts), (0, 2, 1)
    )
    slot_weight = jnp.sum(jnp.where(placing, pair_weight[:, :, None, :], 0.0), axis=3)
    slot_weight = jnp.transpose(slot_weight, (1, 0, 2)).reshape(local_experts, -1)
    return placing.astype(jnp.bfloat16), slot_weight


def body(
    hidden_in,
    queries,
    keys_values,
    request_of_row,
    page_route,
    expert_ids,
    expert_weights,
    norm_gain,
    shared_gate_up,
    shared_down,
    expert_gate_up,
    expert_down,
):
    groups = lax.axis_size("req")
    columns = lax.axis_size("head")
    token_rows = hidden_in.shape[0]
    model_width = hidden_in.shape[1]
    page_rows = token_rows // groups
    group_ids = jnp.arange(groups, dtype=jnp.int32)
    page_dest = page_route.reshape(groups)
    matches = (page_dest[None, :] == group_ids[:, None]).astype(jnp.int32)
    dest_order = jnp.sum(matches * group_ids[None, :], axis=1)

    def by_dest(array_in):
        return jnp.take(array_in.reshape(groups, page_rows, array_in.shape[1]), dest_order, axis=0)

    moved_rows = (
        lax.all_to_all(by_dest(hidden_in), "req", split_axis=0, concat_axis=0, tiled=True),
        lax.all_to_all(by_dest(queries), "req", split_axis=0, concat_axis=0, tiled=True),
        lax.all_to_all(by_dest(keys_values), "req", split_axis=0, concat_axis=0, tiled=True),
    )
    resid = moved_rows[0].reshape(token_rows, model_width)
    rows_of_queries = moved_rows[1].reshape(token_rows, QUERY_HEADS * HEAD_SIZE)
    key_value_rows = moved_rows[2].reshape(token_rows, 2 * KEY_VALUE_HEADS * HEAD_SIZE)
    group_fraction = QUERY_HEADS // KEY_VALUE_HEADS
    key_value_width = KEY_VALUE_HEADS * HEAD_SIZE
    score_scale = HEAD_SIZE ** (-0.5)
    query_start = lax.axis_index("head") * token_rows
    segment_query = lax.dynamic_slice_in_dim(request_of_row, query_start, token_rows)
    position_query = query_start + jnp.arange(token_rows, dtype=jnp.int32)
    query_fourfold = rows_of_queries.reshape(token_rows, KEY_VALUE_HEADS, group_fraction, HEAD_SIZE)
    start_state = (
        jnp.full((KEY_VALUE_HEADS, group_fraction, token_rows), negative_large, jnp.float32),
        jnp.zeros((KEY_VALUE_HEADS, group_fraction, token_rows), jnp.float32),
        jnp.zeros((KEY_VALUE_HEADS, group_fraction, token_rows, HEAD_SIZE), jnp.float32),
    )
    kv_piece = lax.all_gather(key_value_rows, "head", axis=0, tiled=True)
    piece_rows = kv_piece.shape[0]
    rows_per_block = 512

    def one_block(block_index, carried_block):
        offset = block_index * rows_per_block
        current_block = lax.dynamic_slice_in_dim(kv_piece, offset, rows_per_block)
        block_keys = current_block[:, :key_value_width].reshape(
            rows_per_block, KEY_VALUE_HEADS, HEAD_SIZE
        )
        block_values = current_block[:, key_value_width:].reshape(
            rows_per_block, KEY_VALUE_HEADS, HEAD_SIZE
        )
        segment_key = lax.dynamic_slice_in_dim(request_of_row, offset, rows_per_block)
        position_key = offset + jnp.arange(rows_per_block, dtype=jnp.int32)
        allowed = (segment_query[:, None] == segment_key[None, :]) & (
            position_key[None, :] <= position_query[:, None]
        )
        running_max, running_sum, accumulated = carried_block
        score = (
            jnp.einsum(
                "tgqd,sgd->gqts", query_fourfold, block_keys, preferred_element_type=jnp.float32
            )
            * score_scale
        )
        masked = jnp.where(allowed, score, negative_large)
        new_max = jnp.maximum(running_max, jnp.max(masked, axis=-1))
        weights = jnp.where(allowed, jnp.exp(masked - new_max[..., None]), 0.0)
        factor = jnp.exp(running_max - new_max)
        running_sum = running_sum * factor + jnp.sum(weights, axis=-1)
        accumulated = accumulated * factor[..., None] + jnp.einsum(
            "gqts,sgd->gqtd",
            weights.astype(jnp.bfloat16),
            block_values,
            preferred_element_type=jnp.float32,
        )
        return (new_max, running_sum, accumulated)

    running_max, running_sum, accumulated = lax.fori_loop(
        0, piece_rows // rows_per_block, one_block, start_state
    )
    context = jnp.transpose(accumulated / running_sum[..., None], (2, 0, 1, 3)).reshape(
        token_rows, QUERY_HEADS * HEAD_SIZE
    )
    mixed_rows = resid.astype(jnp.float32) + context
    mean_square = jnp.mean(mixed_rows * mixed_rows, axis=1, keepdims=True)
    normed = (mixed_rows * lax.rsqrt(mean_square + 1e-06) * norm_gain).astype(jnp.bfloat16)
    shared_both = jnp.einsum(
        "td,dcf->tcf", normed, shared_gate_up, preferred_element_type=jnp.float32
    )
    shared_hidden = silu_mul(shared_both[:, 0], shared_both[:, 1]).astype(jnp.bfloat16)
    shared_out = jnp.dot(shared_hidden, shared_down, preferred_element_type=jnp.float32)

    all_rows = lax.all_gather(normed, ("req", "head"), axis=0, tiled=True)
    local_experts = expert_gate_up.shape[0]
    placing, slot_weight = slot_tables(
        expert_ids, expert_weights, local_experts, token_rows, groups * columns
    )
    blocks = placing.shape[0]
    slots = placing.shape[2]
    block_rows = placing.shape[3]
    slot_rows = jnp.einsum(
        "bjst,btd->jbsd",
        placing,
        all_rows.reshape(blocks, block_rows, model_width),
        preferred_element_type=jnp.float32,
    ).astype(jnp.bfloat16)
    slot_rows = slot_rows.reshape(local_experts, blocks * slots, model_width)
    gate = jnp.einsum(
        "jsd,jfd->jsf", slot_rows, expert_gate_up[:, 0], preferred_element_type=jnp.float32
    )
    up = jnp.einsum(
        "jsd,jfd->jsf", slot_rows, expert_gate_up[:, 1], preferred_element_type=jnp.float32
    )
    hidden = (silu_mul(gate, up) * slot_weight[:, :, None]).astype(jnp.bfloat16)
    down_out = jnp.einsum(
        "jsf,jfd->jsd", hidden, expert_down, preferred_element_type=jnp.float32
    ).astype(jnp.bfloat16)
    partial_sum = jnp.einsum(
        "bjst,jbsd->btd",
        placing,
        down_out.reshape(local_experts, blocks, slots, model_width),
        preferred_element_type=jnp.float32,
    ).astype(jnp.bfloat16)
    routed = lax.psum_scatter(
        partial_sum.reshape(groups * columns * token_rows, model_width),
        ("req", "head"),
        scatter_dimension=0,
        tiled=True,
    ).astype(jnp.float32)
    return (mixed_rows + shared_out + routed).astype(jnp.bfloat16)


def solution(mesh):
    return jax.shard_map(
        body,
        mesh=mesh,
        in_specs=(
            P(("req", "head"), None),
            P(("req", "head"), None),
            P(("req", "head"), None),
            P("req"),
            P("req", "head", None),
            P(("req", "head"), None),
            P(("req", "head"), None),
            P(),
            P(),
            P(),
            P("head", None, "req", None),
            P("head", "req", None),
        ),
        out_specs=P(("req", "head"), None),
        check_vma=False,
    )
```

```python
import functools

import jax
import jax.numpy as jnp
from jax import lax
from jax.experimental import pallas as pl
from jax.experimental.pallas import tpu as pltpu
from jax.sharding import PartitionSpec as P

QUERY_HEADS = 16
KEY_VALUE_HEADS = 4
HEAD_SIZE = 128
EXPERTS = 32
TOP = 6
CAP = 14


negative_large = -1e30


def silu_mul(gate_value, upward):
    return gate_value / (1.0 + jnp.exp(-gate_value)) * upward


def places():
    r, h = lax.axis_index("req"), lax.axis_index("head")
    return lax.div(r, 2), lax.rem(r, 2), lax.div(h, 2), lax.rem(h, 2)


def partners(zs):
    y, x, z, c = places()
    r, h = y * 2 + x, z * 2 + c
    x_dev = (y * 2 + 1 - x, h)
    y_dev = ((1 - y) * 2 + x, h)
    sibling = (r, z * 2 + 1 - c)
    z_devs = [(r, lax.rem(z + k, zs) * 2 + c) for k in range(zs)]
    return x_dev, y_dev, sibling, z_devs


def greet(devices):
    barrier = pltpu.get_barrier_semaphore()
    for device in devices:
        pl.semaphore_signal(
            barrier, inc=1, device_id=device, device_id_type=pl.DeviceIdType.MESH
        )
    pl.semaphore_wait(barrier, len(devices))


def send(src, dst, send_sem, recv_sem, device):
    return pltpu.make_async_remote_copy(
        src_ref=src,
        dst_ref=dst,
        send_sem=send_sem,
        recv_sem=recv_sem,
        device_id=device,
        device_id_type=pl.DeviceIdType.MESH,
    )


def gather_kernel(zs, n_ref, m_ref, g_ref, w_ref, own, zss, zsr, xs, xr, ys, yr, das, dar, dbs, dbr, ss, sr):
    y, x, z, c = places()
    x_dev, y_dev, sibling, z_devs = partners(zs)
    greet([x_dev, y_dev, sibling] + z_devs[1:])
    pairs = ((n_ref, g_ref), (m_ref, w_ref))
    started = []

    def go(copy):
        copy.start()
        started.append(copy)
        return copy

    local = []
    for a, (src, full) in enumerate(pairs):
        for k in range(1, zs):
            go(send(src, full.at[y, x, z, c], zss.at[a, k], zsr.at[a, k], z_devs[k]))
        copy = pltpu.make_async_copy(src, full.at[y, x, z, c], own.at[a])
        copy.start()
        local.append(copy)

    def arrived(ref, sem):
        send(ref, ref, sem, sem, sibling).wait_recv()

    for step in range(zs + 2):
        if step < zs:
            zk = lax.rem(z - step + zs, zs)
            for a, (src, full) in enumerate(pairs):
                block = full.at[y, x, zk, c]
                if step > 0:
                    arrived(block, zsr.at[a, step])
                    src = block
                go(send(src, block, xs.at[a, step], xr.at[a, step], x_dev))
                go(send(src, block, ys.at[a, step], yr.at[a, step], y_dev))
        if 1 <= step <= zs:
            k = step - 1
            zk = lax.rem(z - k + zs, zs)
            for a, (src, full) in enumerate(pairs):
                half = src.shape[0] // 2
                arrived(full.at[y, 1 - x, zk, c], xr.at[a, k])
                part = full.at[y, 1 - x, zk, c, pl.ds(0, half)]
                go(send(part, part, das.at[a, k], dar.at[a, k], y_dev))
                arrived(full.at[1 - y, x, zk, c], yr.at[a, k])
                part = full.at[1 - y, x, zk, c, pl.ds(half, half)]
                go(send(part, part, dbs.at[a, k], dbr.at[a, k], x_dev))
        if step >= 2:
            k = step - 2
            zk = lax.rem(z - k + zs, zs)
            for a, (src, full) in enumerate(pairs):
                half = src.shape[0] // 2
                if k == 0:
                    local[a].wait()
                arrived(full.at[1 - y, 1 - x, zk, c, pl.ds(0, half)], dar.at[a, k])
                arrived(full.at[1 - y, 1 - x, zk, c, pl.ds(half, half)], dbr.at[a, k])
                part = full.at[:, :, zk, c]
                go(send(part, part, ss.at[a, k], sr.at[a, k], sibling))
    for k in range(zs):
        zk = lax.rem(z - k + zs, zs)
        for a, (src, full) in enumerate(pairs):
            arrived(full.at[:, :, zk, 1 - c], sr.at[a, k])
    for copy in started:
        copy.wait_send()


def gather_all(rows, meta, zs):
    shape = (2, 2, zs, 2)
    sems = pltpu.SemaphoreType.DMA((2, zs))
    return pl.pallas_call(
        functools.partial(gather_kernel, zs),
        out_shape=(
            jax.ShapeDtypeStruct(shape + rows.shape, rows.dtype),
            jax.ShapeDtypeStruct(shape + meta.shape, meta.dtype),
        ),
        in_specs=[pl.BlockSpec(memory_space=pltpu.VMEM)] * 2,
        out_specs=(pl.BlockSpec(memory_space=pl.ANY), pl.BlockSpec(memory_space=pl.ANY)),
        scratch_shapes=[pltpu.SemaphoreType.DMA((2,))] + [sems] * 12,
        compiler_params=pltpu.CompilerParams(
            collective_id=0, has_side_effects=True, vmem_limit_bytes=32 << 20
        ),
    )(rows, meta)


def scatter_kernel(zs, p_ref, o_ref, r1, r2a, r2b, r3a, r3b, s3, r4, sems):
    y, x, z, c = places()
    x_dev, y_dev, sibling, z_devs = partners(zs)
    greet([x_dev, y_dev, sibling] + z_devs[1:])
    rows = o_ref.shape[0]
    half = rows // 2
    strip = 16
    started = []

    def go(src, dst, kind, k, device):
        copy = send(src, dst, sems.at[0, kind, k], sems.at[1, kind, k], device)
        copy.start()
        started.append(copy)
        return copy

    def arrived(ref, kind, k):
        send(ref, ref, sems.at[0, kind, k], sems.at[1, kind, k], sibling).wait_recv()

    for k in range(zs):
        zk = lax.rem(z + 1 + k, zs)
        go(p_ref.at[:, :, zk, 1 - c], r1.at[k], 0, k, sibling)

    for step in range(zs + 2):
        if step < zs:
            k = step
            zk = lax.rem(z + 1 + k, zs)
            arrived(r1.at[k], 0, k)
            strips = rows // strip

            @pl.loop(0, 4 * strips)
            def _(i):
                group = lax.div(i, strips)
                b, a = lax.div(group, 2), lax.rem(group, 2)
                span = pl.ds(lax.rem(i, strips) * strip, strip)
                r1[k, b, a, span, :] = r1[k, b, a, span, :] + p_ref[b, a, zk, c, span, :]

            go(r1.at[k, 1 - y, :, pl.ds(0, half)], r2a.at[k], 1, k, y_dev)
            go(r1.at[k, :, 1 - x, pl.ds(half, half)], r2b.at[k], 2, k, x_dev)
        if 1 <= step <= zs:
            k = step - 1
            strips = half // strip
            arrived(r2a.at[k], 1, k)
            arrived(r2b.at[k], 2, k)

            @pl.loop(0, 2 * strips)
            def _(i):
                a = lax.div(i, strips)
                start = lax.rem(i, strips) * strip
                span, low = pl.ds(start, strip), pl.ds(half + start, strip)
                r2a[k, a, span, :] = r2a[k, a, span, :] + r1[k, y, a, span, :]
                r2b[k, a, span, :] = r2b[k, a, span, :] + r1[k, a, x, low, :]

            go(r2a.at[k, 1 - x], r3a.at[k], 3, k, x_dev)
            go(r2b.at[k, 1 - y], r3b.at[k], 4, k, y_dev)
        if step >= 2:
            k = step - 2
            strips = half // strip
            arrived(r3a.at[k], 3, k)
            arrived(r3b.at[k], 4, k)

            @pl.loop(0, strips)
            def _(i):
                start = i * strip
                span, low = pl.ds(start, strip), pl.ds(half + start, strip)
                s3[k, span, :] = r3a[k, span, :] + r2a[k, x, span, :]
                s3[k, low, :] = r3b[k, span, :] + r2b[k, y, span, :]

            if k < zs - 1:
                go(s3.at[k], r4.at[k], 5, k, z_devs[k + 1])
    for k in range(zs - 1):
        arrived(r4.at[k], 5, k)

    @pl.loop(0, rows // strip)
    def _(i):
        span = pl.ds(i * strip, strip)
        total = s3[zs - 1, span, :].astype(jnp.float32)
        for k in range(zs - 1):
            total = total + r4[k, span, :].astype(jnp.float32)
        o_ref[span, :] = total

    for copy in started:
        copy.wait_send()


def scatter_sum(partial_sum, zs, rows):
    width = partial_sum.shape[-1]
    half = rows // 2
    bf16 = partial_sum.dtype
    return pl.pallas_call(
        functools.partial(scatter_kernel, zs),
        out_shape=jax.ShapeDtypeStruct((rows, width), jnp.float32),
        in_specs=[pl.BlockSpec(memory_space=pltpu.VMEM)],
        out_specs=pl.BlockSpec(memory_space=pltpu.VMEM),
        scratch_shapes=[
            pltpu.VMEM((zs, 2, 2, rows, width), bf16),
            pltpu.VMEM((zs, 2, half, width), bf16),
            pltpu.VMEM((zs, 2, half, width), bf16),
            pltpu.VMEM((zs, half, width), bf16),
            pltpu.VMEM((zs, half, width), bf16),
            pltpu.VMEM((zs, rows, width), bf16),
            pltpu.VMEM((zs - 1, rows, width), bf16),
            pltpu.SemaphoreType.DMA((2, 6, zs)),
        ],
        compiler_params=pltpu.CompilerParams(
            collective_id=1, has_side_effects=True, vmem_limit_bytes=48 << 20
        ),
    )(partial_sum.reshape(2, 2, zs, 2, rows, width))


def slot_tables(all_ids, all_weights, local_experts, token_rows, devices):
    first = lax.axis_index("head") * local_experts
    mine = first + jnp.arange(local_experts, dtype=jnp.int32)
    hit = all_ids[:, :, None] == mine[None, None, :]
    pair_weight = jnp.sum(jnp.where(hit, all_weights[:, :, None], 0.0), axis=1)
    named = jnp.any(hit, axis=1).reshape(devices, token_rows, local_experts)
    before = jnp.tril(jnp.ones((token_rows, token_rows), jnp.bfloat16), -1)
    rank = jnp.einsum(
        "ut,dtj->duj", before, named.astype(jnp.bfloat16), preferred_element_type=jnp.float32
    ).astype(jnp.int32)
    joined = 4
    blocks = devices // joined
    place = jnp.arange(devices, dtype=jnp.int32)[:, None, None] % joined * CAP + rank
    place = jnp.where(named, place, -1).reshape(blocks, joined * token_rows, local_experts)
    place = jnp.transpose(place, (0, 2, 1))
    slots = jnp.arange(joined * CAP, dtype=jnp.int32)
    placing = place[:, :, None, :] == slots[None, None, :, None]
    pair_weight = jnp.transpose(
        pair_weight.reshape(blocks, joined * token_rows, local_experts), (0, 2, 1)
    )
    slot_weight = jnp.sum(jnp.where(placing, pair_weight[:, :, None, :], 0.0), axis=3)
    slot_weight = jnp.transpose(slot_weight, (1, 0, 2)).reshape(local_experts, -1)
    return placing.astype(jnp.bfloat16), slot_weight


def body(
    hidden_in,
    queries,
    keys_values,
    request_of_row,
    page_route,
    expert_ids,
    expert_weights,
    norm_gain,
    shared_gate_up,
    shared_down,
    expert_gate_up,
    expert_down,
):
    groups = lax.axis_size("req")
    columns = lax.axis_size("head")
    token_rows = hidden_in.shape[0]
    model_width = hidden_in.shape[1]
    page_rows = token_rows // groups
    group_ids = jnp.arange(groups, dtype=jnp.int32)
    page_dest = page_route.reshape(groups)
    matches = (page_dest[None, :] == group_ids[:, None]).astype(jnp.int32)
    dest_order = jnp.sum(matches * group_ids[None, :], axis=1)

    def by_dest(array_in):
        return jnp.take(array_in.reshape(groups, page_rows, array_in.shape[1]), dest_order, axis=0)

    moved_rows = (
        lax.all_to_all(by_dest(hidden_in), "req", split_axis=0, concat_axis=0, tiled=True),
        lax.all_to_all(by_dest(queries), "req", split_axis=0, concat_axis=0, tiled=True),
        lax.all_to_all(by_dest(keys_values), "req", split_axis=0, concat_axis=0, tiled=True),
    )
    resid = moved_rows[0].reshape(token_rows, model_width)
    rows_of_queries = moved_rows[1].reshape(token_rows, QUERY_HEADS * HEAD_SIZE)
    key_value_rows = moved_rows[2].reshape(token_rows, 2 * KEY_VALUE_HEADS * HEAD_SIZE)
    group_fraction = QUERY_HEADS // KEY_VALUE_HEADS
    key_value_width = KEY_VALUE_HEADS * HEAD_SIZE
    score_scale = HEAD_SIZE ** (-0.5)
    query_start = lax.axis_index("head") * token_rows
    segment_query = lax.dynamic_slice_in_dim(request_of_row, query_start, token_rows)
    position_query = query_start + jnp.arange(token_rows, dtype=jnp.int32)
    query_fourfold = rows_of_queries.reshape(token_rows, KEY_VALUE_HEADS, group_fraction, HEAD_SIZE)
    start_state = (
        jnp.full((KEY_VALUE_HEADS, group_fraction, token_rows), negative_large, jnp.float32),
        jnp.zeros((KEY_VALUE_HEADS, group_fraction, token_rows), jnp.float32),
        jnp.zeros((KEY_VALUE_HEADS, group_fraction, token_rows, HEAD_SIZE), jnp.float32),
    )
    kv_piece = lax.all_gather(key_value_rows, "head", axis=0, tiled=True)
    piece_rows = kv_piece.shape[0]
    rows_per_block = 512

    def one_block(block_index, carried_block):
        offset = block_index * rows_per_block
        current_block = lax.dynamic_slice_in_dim(kv_piece, offset, rows_per_block)
        block_keys = current_block[:, :key_value_width].reshape(
            rows_per_block, KEY_VALUE_HEADS, HEAD_SIZE
        )
        block_values = current_block[:, key_value_width:].reshape(
            rows_per_block, KEY_VALUE_HEADS, HEAD_SIZE
        )
        segment_key = lax.dynamic_slice_in_dim(request_of_row, offset, rows_per_block)
        position_key = offset + jnp.arange(rows_per_block, dtype=jnp.int32)
        allowed = (segment_query[:, None] == segment_key[None, :]) & (
            position_key[None, :] <= position_query[:, None]
        )
        running_max, running_sum, accumulated = carried_block
        score = (
            jnp.einsum(
                "tgqd,sgd->gqts", query_fourfold, block_keys, preferred_element_type=jnp.float32
            )
            * score_scale
        )
        masked = jnp.where(allowed, score, negative_large)
        new_max = jnp.maximum(running_max, jnp.max(masked, axis=-1))
        weights = jnp.where(allowed, jnp.exp(masked - new_max[..., None]), 0.0)
        factor = jnp.exp(running_max - new_max)
        running_sum = running_sum * factor + jnp.sum(weights, axis=-1)
        accumulated = accumulated * factor[..., None] + jnp.einsum(
            "gqts,sgd->gqtd",
            weights.astype(jnp.bfloat16),
            block_values,
            preferred_element_type=jnp.float32,
        )
        return (new_max, running_sum, accumulated)

    running_max, running_sum, accumulated = lax.fori_loop(
        0, piece_rows // rows_per_block, one_block, start_state
    )
    context = jnp.transpose(accumulated / running_sum[..., None], (2, 0, 1, 3)).reshape(
        token_rows, QUERY_HEADS * HEAD_SIZE
    )
    mixed_rows = resid.astype(jnp.float32) + context
    mean_square = jnp.mean(mixed_rows * mixed_rows, axis=1, keepdims=True)
    normed = (mixed_rows * lax.rsqrt(mean_square + 1e-06) * norm_gain).astype(jnp.bfloat16)
    shared_both = jnp.einsum(
        "td,dcf->tcf", normed, shared_gate_up, preferred_element_type=jnp.float32
    )
    shared_hidden = silu_mul(shared_both[:, 0], shared_both[:, 1]).astype(jnp.bfloat16)
    shared_out = jnp.dot(shared_hidden, shared_down, preferred_element_type=jnp.float32)

    devices = groups * columns
    by_kernel = groups == 4 and columns * groups * normed.size * 2 <= 16 << 20
    if by_kernel:
        meta = jnp.concatenate([expert_ids.astype(jnp.float32), expert_weights], axis=1).T
        meta = jnp.pad(meta, ((0, 16 - 2 * TOP), (0, -token_rows % 128)))
        all_rows, all_meta = gather_all(normed, meta, columns // 2)
        all_meta = all_meta.reshape(devices, meta.shape[0], meta.shape[1])[:, :, :token_rows]
        all_meta = jnp.transpose(all_meta, (0, 2, 1)).reshape(devices * token_rows, -1)
        all_ids = all_meta[:, :TOP].astype(jnp.int32)
        all_weights = all_meta[:, TOP : 2 * TOP]
    else:
        all_rows = lax.all_gather(normed, ("req", "head"), axis=0, tiled=True)
        all_ids = lax.all_gather(expert_ids, ("req", "head"), axis=0, tiled=True)
        all_weights = lax.all_gather(expert_weights, ("req", "head"), axis=0, tiled=True)
    local_experts = expert_gate_up.shape[0]
    placing, slot_weight = slot_tables(
        all_ids, all_weights, local_experts, token_rows, devices
    )
    blocks = placing.shape[0]
    slots = placing.shape[2]
    block_rows = placing.shape[3]
    slot_rows = jnp.einsum(
        "bjst,btd->jbsd",
        placing,
        all_rows.reshape(blocks, block_rows, model_width),
        preferred_element_type=jnp.float32,
    ).astype(jnp.bfloat16)
    slot_rows = slot_rows.reshape(local_experts, blocks * slots, model_width)
    gate = jnp.einsum(
        "jsd,jfd->jsf", slot_rows, expert_gate_up[:, 0], preferred_element_type=jnp.float32
    )
    up = jnp.einsum(
        "jsd,jfd->jsf", slot_rows, expert_gate_up[:, 1], preferred_element_type=jnp.float32
    )
    hidden = (silu_mul(gate, up) * slot_weight[:, :, None]).astype(jnp.bfloat16)
    down_out = jnp.einsum(
        "jsf,jfd->jsd", hidden, expert_down, preferred_element_type=jnp.float32
    ).astype(jnp.bfloat16)
    partial_sum = jnp.einsum(
        "bjst,jbsd->btd",
        placing,
        down_out.reshape(local_experts, blocks, slots, model_width),
        preferred_element_type=jnp.float32,
    ).astype(jnp.bfloat16)
    if by_kernel:
        routed = scatter_sum(partial_sum, columns // 2, token_rows)
    else:
        routed = lax.psum_scatter(
            partial_sum.reshape(devices * token_rows, model_width),
            ("req", "head"),
            scatter_dimension=0,
            tiled=True,
        ).astype(jnp.float32)
    return (mixed_rows + shared_out + routed).astype(jnp.bfloat16)


def solution(mesh):
    return jax.shard_map(
        body,
        mesh=mesh,
        in_specs=(
            P(("req", "head"), None),
            P(("req", "head"), None),
            P(("req", "head"), None),
            P("req"),
            P("req", "head", None),
            P(("req", "head"), None),
            P(("req", "head"), None),
            P(),
            P(),
            P(),
            P("head", None, "req", None),
            P("head", "req", None),
        ),
        out_specs=P(("req", "head"), None),
        check_vma=False,
    )
```

```python
import functools

import jax
import jax.numpy as jnp
from jax import lax
from jax.experimental import pallas as pl
from jax.experimental.pallas import tpu as pltpu
from jax.sharding import PartitionSpec as P

QUERY_HEADS = 16
KEY_VALUE_HEADS = 4
HEAD_SIZE = 128
EXPERTS = 32
TOP = 6
CAP = 14


negative_large = -1e30


def silu_mul(gate_value, upward):
    return gate_value / (1.0 + jnp.exp(-gate_value)) * upward


def places():
    r, h = lax.axis_index("req"), lax.axis_index("head")
    return lax.div(r, 2), lax.rem(r, 2), lax.div(h, 2), lax.rem(h, 2)


def partners(zs):
    y, x, z, c = places()
    r, h = y * 2 + x, z * 2 + c
    x_dev = (y * 2 + 1 - x, h)
    y_dev = ((1 - y) * 2 + x, h)
    sibling = (r, z * 2 + 1 - c)
    z_devs = [(r, lax.rem(z + k, zs) * 2 + c) for k in range(zs)]
    return x_dev, y_dev, sibling, z_devs


def greet(devices):
    barrier = pltpu.get_barrier_semaphore()
    for device in devices:
        pl.semaphore_signal(
            barrier, inc=1, device_id=device, device_id_type=pl.DeviceIdType.MESH
        )
    pl.semaphore_wait(barrier, len(devices))


def send(src, dst, send_sem, recv_sem, device):
    return pltpu.make_async_remote_copy(
        src_ref=src,
        dst_ref=dst,
        send_sem=send_sem,
        recv_sem=recv_sem,
        device_id=device,
        device_id_type=pl.DeviceIdType.MESH,
    )


def gather_kernel(zs, n_ref, m_ref, g_ref, w_ref, own, zss, zsr, xs, xr, ys, yr, das, dar, dbs, dbr, ss, sr):
    y, x, z, c = places()
    x_dev, y_dev, sibling, z_devs = partners(zs)
    greet([x_dev, y_dev, sibling] + z_devs[1:])
    pairs = ((n_ref, g_ref), (m_ref, w_ref))
    started = []

    def go(copy):
        copy.start()
        started.append(copy)
        return copy

    local = []
    for a, (src, full) in enumerate(pairs):
        for k in range(1, zs):
            go(send(src, full.at[y, x, z, c], zss.at[a, k], zsr.at[a, k], z_devs[k]))
        copy = pltpu.make_async_copy(src, full.at[y, x, z, c], own.at[a])
        copy.start()
        local.append(copy)

    def arrived(ref, sem):
        send(ref, ref, sem, sem, sibling).wait_recv()

    for step in range(zs + 2):
        if step < zs:
            zk = lax.rem(z - step + zs, zs)
            for a, (src, full) in enumerate(pairs):
                block = full.at[y, x, zk, c]
                if step > 0:
                    arrived(block, zsr.at[a, step])
                    src = block
                go(send(src, block, xs.at[a, step], xr.at[a, step], x_dev))
                go(send(src, block, ys.at[a, step], yr.at[a, step], y_dev))
        if 1 <= step <= zs:
            k = step - 1
            zk = lax.rem(z - k + zs, zs)
            for a, (src, full) in enumerate(pairs):
                half = src.shape[0] // 2
                arrived(full.at[y, 1 - x, zk, c], xr.at[a, k])
                part = full.at[y, 1 - x, zk, c, pl.ds(0, half)]
                go(send(part, part, das.at[a, k], dar.at[a, k], y_dev))
                arrived(full.at[1 - y, x, zk, c], yr.at[a, k])
                part = full.at[1 - y, x, zk, c, pl.ds(half, half)]
                go(send(part, part, dbs.at[a, k], dbr.at[a, k], x_dev))
        if step >= 2:
            k = step - 2
            zk = lax.rem(z - k + zs, zs)
            for a, (src, full) in enumerate(pairs):
                half = src.shape[0] // 2
                if k == 0:
                    local[a].wait()
                arrived(full.at[1 - y, 1 - x, zk, c, pl.ds(0, half)], dar.at[a, k])
                arrived(full.at[1 - y, 1 - x, zk, c, pl.ds(half, half)], dbr.at[a, k])
                part = full.at[:, :, zk, c]
                go(send(part, part, ss.at[a, k], sr.at[a, k], sibling))
    for k in range(zs):
        zk = lax.rem(z - k + zs, zs)
        for a, (src, full) in enumerate(pairs):
            arrived(full.at[:, :, zk, 1 - c], sr.at[a, k])
    for copy in started:
        copy.wait_send()


def gather_all(rows, meta, zs):
    shape = (2, 2, zs, 2)
    sems = pltpu.SemaphoreType.DMA((2, zs))
    return pl.pallas_call(
        functools.partial(gather_kernel, zs),
        out_shape=(
            jax.ShapeDtypeStruct(shape + rows.shape, rows.dtype),
            jax.ShapeDtypeStruct(shape + meta.shape, meta.dtype),
        ),
        in_specs=[pl.BlockSpec(memory_space=pltpu.VMEM)] * 2,
        out_specs=(pl.BlockSpec(memory_space=pl.ANY), pl.BlockSpec(memory_space=pl.ANY)),
        scratch_shapes=[pltpu.SemaphoreType.DMA((2,))] + [sems] * 12,
        compiler_params=pltpu.CompilerParams(
            collective_id=0, has_side_effects=True, vmem_limit_bytes=32 << 20
        ),
    )(rows, meta)


def scatter_kernel(zs, p_ref, o_ref, r1, r2a, r2b, r3a, r3b, s3, r4, sems):
    y, x, z, c = places()
    x_dev, y_dev, sibling, z_devs = partners(zs)
    greet([x_dev, y_dev, sibling] + z_devs[1:])
    rows = o_ref.shape[0]
    half = rows // 2
    strip = 16
    started = []

    def go(src, dst, kind, k, device):
        copy = send(src, dst, sems.at[0, kind, k], sems.at[1, kind, k], device)
        copy.start()
        started.append(copy)
        return copy

    def arrived(ref, kind, k):
        send(ref, ref, sems.at[0, kind, k], sems.at[1, kind, k], sibling).wait_recv()

    for k in range(zs):
        zk = lax.rem(z + 1 + k, zs)
        go(p_ref.at[:, :, zk, 1 - c], r1.at[k], 0, k, sibling)

    for step in range(zs + 2):
        if step < zs:
            k = step
            zk = lax.rem(z + 1 + k, zs)
            arrived(r1.at[k], 0, k)
            strips = rows // strip

            @pl.loop(0, 4 * strips)
            def _(i):
                group = lax.div(i, strips)
                b, a = lax.div(group, 2), lax.rem(group, 2)
                span = pl.ds(lax.rem(i, strips) * strip, strip)
                r1[k, b, a, span, :] = r1[k, b, a, span, :] + p_ref[b, a, zk, c, span, :]

            go(r1.at[k, 1 - y, :, pl.ds(0, half)], r2a.at[k], 1, k, y_dev)
            go(r1.at[k, :, 1 - x, pl.ds(half, half)], r2b.at[k], 2, k, x_dev)
        if 1 <= step <= zs:
            k = step - 1
            strips = half // strip
            arrived(r2a.at[k], 1, k)
            arrived(r2b.at[k], 2, k)

            @pl.loop(0, 2 * strips)
            def _(i):
                a = lax.div(i, strips)
                start = lax.rem(i, strips) * strip
                span, low = pl.ds(start, strip), pl.ds(half + start, strip)
                r2a[k, a, span, :] = r2a[k, a, span, :] + r1[k, y, a, span, :]
                r2b[k, a, span, :] = r2b[k, a, span, :] + r1[k, a, x, low, :]

            go(r2a.at[k, 1 - x], r3a.at[k], 3, k, x_dev)
            go(r2b.at[k, 1 - y], r3b.at[k], 4, k, y_dev)
        if step >= 2:
            k = step - 2
            strips = half // strip
            arrived(r3a.at[k], 3, k)
            arrived(r3b.at[k], 4, k)

            @pl.loop(0, strips)
            def _(i):
                start = i * strip
                span, low = pl.ds(start, strip), pl.ds(half + start, strip)
                s3[k, span, :] = r3a[k, span, :] + r2a[k, x, span, :]
                s3[k, low, :] = r3b[k, span, :] + r2b[k, y, span, :]

            if k < zs - 1:
                go(s3.at[k], r4.at[k], 5, k, z_devs[k + 1])
    for k in range(zs - 1):
        arrived(r4.at[k], 5, k)

    @pl.loop(0, rows // strip)
    def _(i):
        span = pl.ds(i * strip, strip)
        total = s3[zs - 1, span, :].astype(jnp.float32)
        for k in range(zs - 1):
            total = total + r4[k, span, :].astype(jnp.float32)
        o_ref[span, :] = total

    for copy in started:
        copy.wait_send()


def scatter_sum(partial_sum, zs, rows):
    width = partial_sum.shape[-1]
    half = rows // 2
    bf16 = partial_sum.dtype
    return pl.pallas_call(
        functools.partial(scatter_kernel, zs),
        out_shape=jax.ShapeDtypeStruct((rows, width), jnp.float32),
        in_specs=[pl.BlockSpec(memory_space=pltpu.VMEM)],
        out_specs=pl.BlockSpec(memory_space=pltpu.VMEM),
        scratch_shapes=[
            pltpu.VMEM((zs, 2, 2, rows, width), bf16),
            pltpu.VMEM((zs, 2, half, width), bf16),
            pltpu.VMEM((zs, 2, half, width), bf16),
            pltpu.VMEM((zs, half, width), bf16),
            pltpu.VMEM((zs, half, width), bf16),
            pltpu.VMEM((zs, rows, width), bf16),
            pltpu.VMEM((zs - 1, rows, width), bf16),
            pltpu.SemaphoreType.DMA((2, 6, zs)),
        ],
        compiler_params=pltpu.CompilerParams(
            collective_id=1, has_side_effects=True, vmem_limit_bytes=48 << 20
        ),
    )(partial_sum.reshape(2, 2, zs, 2, rows, width))


def slot_tables(all_ids, all_weights, local_experts, token_rows, devices):
    first = lax.axis_index("head") * local_experts
    mine = first + jnp.arange(local_experts, dtype=jnp.int32)
    hit = all_ids[:, :, None] == mine[None, None, :]
    pair_weight = jnp.sum(jnp.where(hit, all_weights[:, :, None], 0.0), axis=1)
    named = jnp.any(hit, axis=1).reshape(devices, token_rows, local_experts)
    before = jnp.tril(jnp.ones((token_rows, token_rows), jnp.bfloat16), -1)
    rank = jnp.einsum(
        "ut,dtj->duj", before, named.astype(jnp.bfloat16), preferred_element_type=jnp.float32
    ).astype(jnp.int32)
    joined = 8
    blocks = devices // joined
    place = jnp.arange(devices, dtype=jnp.int32)[:, None, None] % joined * CAP + rank
    place = jnp.where(named, place, -1).reshape(blocks, joined * token_rows, local_experts)
    place = jnp.transpose(place, (0, 2, 1))
    slots = jnp.arange(joined * CAP, dtype=jnp.int32)
    placing = place[:, :, None, :] == slots[None, None, :, None]
    pair_weight = jnp.transpose(
        pair_weight.reshape(blocks, joined * token_rows, local_experts), (0, 2, 1)
    )
    slot_weight = jnp.sum(jnp.where(placing, pair_weight[:, :, None, :], 0.0), axis=3)
    slot_weight = jnp.transpose(slot_weight, (1, 0, 2)).reshape(local_experts, -1)
    return placing.astype(jnp.bfloat16), slot_weight


def body(
    hidden_in,
    queries,
    keys_values,
    request_of_row,
    page_route,
    expert_ids,
    expert_weights,
    norm_gain,
    shared_gate_up,
    shared_down,
    expert_gate_up,
    expert_down,
):
    groups = lax.axis_size("req")
    columns = lax.axis_size("head")
    token_rows = hidden_in.shape[0]
    model_width = hidden_in.shape[1]
    page_rows = token_rows // groups
    group_ids = jnp.arange(groups, dtype=jnp.int32)
    page_dest = page_route.reshape(groups)
    matches = (page_dest[None, :] == group_ids[:, None]).astype(jnp.int32)
    dest_order = jnp.sum(matches * group_ids[None, :], axis=1)

    def by_dest(array_in):
        return jnp.take(array_in.reshape(groups, page_rows, array_in.shape[1]), dest_order, axis=0)

    moved_rows = (
        lax.all_to_all(by_dest(hidden_in), "req", split_axis=0, concat_axis=0, tiled=True),
        lax.all_to_all(by_dest(queries), "req", split_axis=0, concat_axis=0, tiled=True),
        lax.all_to_all(by_dest(keys_values), "req", split_axis=0, concat_axis=0, tiled=True),
    )
    resid = moved_rows[0].reshape(token_rows, model_width)
    rows_of_queries = moved_rows[1].reshape(token_rows, QUERY_HEADS * HEAD_SIZE)
    key_value_rows = moved_rows[2].reshape(token_rows, 2 * KEY_VALUE_HEADS * HEAD_SIZE)
    group_fraction = QUERY_HEADS // KEY_VALUE_HEADS
    key_value_width = KEY_VALUE_HEADS * HEAD_SIZE
    score_scale = HEAD_SIZE ** (-0.5)
    query_start = lax.axis_index("head") * token_rows
    segment_query = lax.dynamic_slice_in_dim(request_of_row, query_start, token_rows)
    position_query = query_start + jnp.arange(token_rows, dtype=jnp.int32)
    query_fourfold = rows_of_queries.reshape(token_rows, KEY_VALUE_HEADS, group_fraction, HEAD_SIZE)
    start_state = (
        jnp.full((KEY_VALUE_HEADS, group_fraction, token_rows), negative_large, jnp.float32),
        jnp.zeros((KEY_VALUE_HEADS, group_fraction, token_rows), jnp.float32),
        jnp.zeros((KEY_VALUE_HEADS, group_fraction, token_rows, HEAD_SIZE), jnp.float32),
    )
    kv_piece = lax.all_gather(key_value_rows, "head", axis=0, tiled=True)
    piece_rows = kv_piece.shape[0]
    rows_per_block = 512

    def one_block(block_index, carried_block):
        offset = block_index * rows_per_block
        current_block = lax.dynamic_slice_in_dim(kv_piece, offset, rows_per_block)
        block_keys = current_block[:, :key_value_width].reshape(
            rows_per_block, KEY_VALUE_HEADS, HEAD_SIZE
        )
        block_values = current_block[:, key_value_width:].reshape(
            rows_per_block, KEY_VALUE_HEADS, HEAD_SIZE
        )
        segment_key = lax.dynamic_slice_in_dim(request_of_row, offset, rows_per_block)
        position_key = offset + jnp.arange(rows_per_block, dtype=jnp.int32)
        allowed = (segment_query[:, None] == segment_key[None, :]) & (
            position_key[None, :] <= position_query[:, None]
        )
        running_max, running_sum, accumulated = carried_block
        score = (
            jnp.einsum(
                "tgqd,sgd->gqts", query_fourfold, block_keys, preferred_element_type=jnp.float32
            )
            * score_scale
        )
        masked = jnp.where(allowed, score, negative_large)
        new_max = jnp.maximum(running_max, jnp.max(masked, axis=-1))
        weights = jnp.where(allowed, jnp.exp(masked - new_max[..., None]), 0.0)
        factor = jnp.exp(running_max - new_max)
        running_sum = running_sum * factor + jnp.sum(weights, axis=-1)
        accumulated = accumulated * factor[..., None] + jnp.einsum(
            "gqts,sgd->gqtd",
            weights.astype(jnp.bfloat16),
            block_values,
            preferred_element_type=jnp.float32,
        )
        return (new_max, running_sum, accumulated)

    running_max, running_sum, accumulated = lax.fori_loop(
        0, piece_rows // rows_per_block, one_block, start_state
    )
    context = jnp.transpose(accumulated / running_sum[..., None], (2, 0, 1, 3)).reshape(
        token_rows, QUERY_HEADS * HEAD_SIZE
    )
    mixed_rows = resid.astype(jnp.float32) + context
    mean_square = jnp.mean(mixed_rows * mixed_rows, axis=1, keepdims=True)
    normed = (mixed_rows * lax.rsqrt(mean_square + 1e-06) * norm_gain).astype(jnp.bfloat16)
    shared_both = jnp.einsum(
        "td,dcf->tcf", normed, shared_gate_up, preferred_element_type=jnp.float32
    )
    shared_hidden = silu_mul(shared_both[:, 0], shared_both[:, 1]).astype(jnp.bfloat16)
    shared_out = jnp.dot(shared_hidden, shared_down, preferred_element_type=jnp.float32)

    devices = groups * columns
    by_kernel = groups == 4 and columns * groups * normed.size * 2 <= 16 << 20
    if by_kernel:
        meta = jnp.concatenate([expert_ids.astype(jnp.float32), expert_weights], axis=1).T
        meta = jnp.pad(meta, ((0, 16 - 2 * TOP), (0, -token_rows % 128)))
        all_rows, all_meta = gather_all(normed, meta, columns // 2)
        all_meta = all_meta.reshape(devices, meta.shape[0], meta.shape[1])[:, :, :token_rows]
        all_meta = jnp.transpose(all_meta, (0, 2, 1)).reshape(devices * token_rows, -1)
        all_ids = all_meta[:, :TOP].astype(jnp.int32)
        all_weights = all_meta[:, TOP : 2 * TOP]
    else:
        all_rows = lax.all_gather(normed, ("req", "head"), axis=0, tiled=True)
        all_ids = lax.all_gather(expert_ids, ("req", "head"), axis=0, tiled=True)
        all_weights = lax.all_gather(expert_weights, ("req", "head"), axis=0, tiled=True)
    local_experts = expert_gate_up.shape[0]
    placing, slot_weight = slot_tables(
        all_ids, all_weights, local_experts, token_rows, devices
    )
    blocks = placing.shape[0]
    slots = placing.shape[2]
    block_rows = placing.shape[3]
    slot_rows = jnp.einsum(
        "bjst,btd->jbsd",
        placing,
        all_rows.reshape(blocks, block_rows, model_width),
        preferred_element_type=jnp.float32,
    ).astype(jnp.bfloat16)
    slot_rows = slot_rows.reshape(local_experts, blocks * slots, model_width)
    gate = jnp.einsum(
        "jsd,jfd->jsf", slot_rows, expert_gate_up[:, 0], preferred_element_type=jnp.float32
    )
    up = jnp.einsum(
        "jsd,jfd->jsf", slot_rows, expert_gate_up[:, 1], preferred_element_type=jnp.float32
    )
    hidden = (silu_mul(gate, up) * slot_weight[:, :, None]).astype(jnp.bfloat16)
    down_out = jnp.einsum(
        "jsf,jfd->jsd", hidden, expert_down, preferred_element_type=jnp.float32
    ).astype(jnp.bfloat16)
    partial_sum = jnp.einsum(
        "bjst,jbsd->btd",
        placing,
        down_out.reshape(local_experts, blocks, slots, model_width),
        preferred_element_type=jnp.float32,
    ).astype(jnp.bfloat16)
    if by_kernel:
        routed = scatter_sum(partial_sum, columns // 2, token_rows)
    else:
        routed = lax.psum_scatter(
            partial_sum.reshape(devices * token_rows, model_width),
            ("req", "head"),
            scatter_dimension=0,
            tiled=True,
        ).astype(jnp.float32)
    return (mixed_rows + shared_out + routed).astype(jnp.bfloat16)


def solution(mesh):
    return jax.shard_map(
        body,
        mesh=mesh,
        in_specs=(
            P(("req", "head"), None),
            P(("req", "head"), None),
            P(("req", "head"), None),
            P("req"),
            P("req", "head", None),
            P(("req", "head"), None),
            P(("req", "head"), None),
            P(),
            P(),
            P(),
            P("head", None, "req", None),
            P("head", "req", None),
        ),
        out_specs=P(("req", "head"), None),
        check_vma=False,
    )
```
